32 devices in a mesh: groups: 2 (over x), blocks: 16 (over z, y, core).
Axes of the slice: x: 2, y: 2, z: 4, core: 2. Of those that a mesh axis runs over, the one named last changes fastest.
Arguments:
- probes: bfloat16 [8192, 256], P(('groups', 'blocks')), parts along dimension 0, may hold values from -4 to 4
- cheb_coef: float32 [10], P('groups'), parts along dimension 0, may hold values from 0.5 to 1.5
- col_basis: bfloat16 [8192, 64], P(('groups', 'blocks')), parts along dimension 0, may hold values from -0.375 to 0.375
- row_basis: bfloat16 [8192, 64], P(('groups', 'blocks')), parts along dimension 0, may hold values from -0.0234375 to 0.0234375
- near_tiles: bfloat16 [8192, 768], P(('groups', 'blocks')), parts along dimension 0, may hold values from -0.0546875 to 0.0546875
- coupling: bfloat16 [2048, 64, 64], P(('groups', 'blocks')), parts along dimension 0, may hold values from -0.75 to 0.75
- far_rows: int32 [2048, 1], P(('groups', 'blocks')), parts along dimension 0, may hold values from 0 to 15; in each aligned block of 64 rows (0 to 63, 64 to 127, ...) at most 8 rows name the same one
- far_cols: int32 [2048], P(('groups', 'blocks')), parts along dimension 0, may hold values from 0 to 15
Outputs:
- estimate: float32 [8192, 256], P(('groups', 'blocks')), parts along dimension 0
The draws below stay inside these ranges and needn't reach their ends.
There are 2 independent parts, one for each index of `groups`. The reference program is written for one: setup_inputs(seed, part) draws one part's arguments, and reference() takes and returns one part's arrays. A program takes and returns all parts, laid end to end along the dimension named above; each array names one. Nothing has to cross between parts.
Inputs may be any that keep to these rules, and one draw needn't show every extreme that they name: `far_rows`: cluster r is the rows r * 256 onward. Among the 64 coupling blocks of one device at most 8 share a row cluster, and that many do on some device.
All inputs are finite; a program needn't handle non-finite values.
Results may differ from the reference program's by a relative error of at most 0.0085.
Values may be sent and summed in bfloat16 or wider, within the bound.
A program may use at most 64 MiB of HBM per device.

```python
import math
import jax
import jax.numpy as jnp
import numpy as np
from jax import lax

CLUSTER = 256
RANK = 64
PROBES = 256
ITERS = 4
LEAF_DEV = 64
CLUSTERS = 16
POINTS = 4096
LEAVES = 1024
SLOT_CAP = 8
N_BLOCKS = 16


def touch_ends(drawn, rng, least, high):
    extent = drawn.shape
    spot = [jax.random.randint(jax.random.fold_in(rng, axis), (), 0, extent[axis]) for axis in range(len(extent))]
    drawn = drawn.at[tuple(spot)].set(least)
    longest = extent.index(max(extent))
    spot[longest] = (spot[longest] + 1) % extent[longest]
    return drawn.at[tuple(spot)].set(high)


def block_levels(key, shape, split, smallest, top_value):
    def one(axis_at, blocks):
        heights = jax.random.uniform(jax.random.fold_in(jax.random.fold_in(key, 6), axis_at), (blocks,), jnp.float32, smallest / len(split), top_value / len(split))
        return jnp.repeat(jnp.exp(heights), shape[axis_at] // blocks).reshape((-1,) + (1,) * (len(shape) - axis_at - 1))

    gain = one(*split[0])
    for cut in split[1:]:
        gain = gain * one(*cut)
    return gain


def deal_out(own_key, own, number, rows, amount, top, reach, skew):
    order = jax.random.permutation(own_key, amount)
    packed, usual = portions_of(amount, rows * top, reach, skew, True), portions_of(amount, rows * top, reach, skew, False)
    places = jnp.arange(amount)

    def named(sizes, rotation):
        used = int((sizes > 0).sum())
        fixed = max(1, used // 4)
        moved = fixed + (places - fixed + rotation * (used - fixed)) % max(1, amount - fixed)
        return jnp.zeros((amount,), jnp.int32).at[order[jnp.where(places < fixed, places, moved)]].set(jnp.asarray(sizes, jnp.int32))

    sizes = jnp.where(number % 4 == 0, named(packed, number // 4), named(usual, number - number // 4 - 1))
    mixed = jax.random.permutation(jax.random.fold_in(own, 3), amount)
    source_of, taker = mixed[0:amount // 2 * 2:2], mixed[1:amount // 2 * 2:2]
    room = jnp.minimum(sizes[source_of] - 1, reach - sizes[taker]) // 2
    room = jnp.where((source_of == order[0]) | (taker == order[0]) | (sizes[taker] == 0), 0, jnp.maximum(room, 0))
    moved = jax.random.randint(jax.random.fold_in(own, 4), (amount // 2,), 0, 1 << 20) % (room + 1)
    sizes = sizes.at[source_of].add(-moved).at[taker].add(moved)
    labels = jnp.searchsorted(jnp.cumsum(sizes), jnp.arange(rows * top), side="right").astype(jnp.int32)
    listing = labels.reshape(top, rows).T
    listing = listing[jax.random.permutation(jax.random.fold_in(own, 1), rows)]
    rotation = jax.random.randint(jax.random.fold_in(own, 2), (rows, 1), 0, top)
    return jnp.take_along_axis(listing, (jnp.arange(top)[None, :] + rotation) % top, axis=1)


def portions_of(number_of, total, reach, lean, full):
    loads = [(1 << 20) // math.isqrt(rank ** lean) + 1 for rank in range(1, number_of + 1)]
    largest = reach if full else min(reach, max(-(-total // number_of), total * loads[0] // sum(loads)))
    least = 1 if total - largest >= number_of - 1 else 0
    holding, spare = [largest] + [least] * (number_of - 1), total - largest - least * (number_of - 1)
    while spare > 0:
        free = [i for i in range(1, number_of) if holding[i] < largest] or [i for i in range(1, number_of) if holding[i] < reach]
        whole, left = sum([loads[i] for i in free]), spare
        for i in free:
            addition = min(reach - holding[i], max(1, left * loads[i] // whole), spare)
            holding[i] = holding[i] + addition
            spare = spare - addition
    return np.array(holding)


def centred(own_key, shape, spread, limit, pieces=(), kind=jnp.bfloat16):
    array = spread * jax.random.normal(own_key, shape, jnp.float32)
    if pieces:
        array = array * block_levels(own_key, shape, pieces, -0.22, 0.18)
    return jnp.clip(array, -limit, limit).astype(kind)


def setup_inputs(seed: int = 0, part: int = 0) -> dict:
    key_list = jax.random.split(jax.random.key(seed), 9)
    part_splits = jax.random.split(jax.random.fold_in(key_list[8], part), 9)
    probes = centred(part_splits[0], (POINTS, PROBES), 1.0, 4.0, ((0, 16),))
    cheb_coef = jnp.clip(jax.random.uniform(part_splits[1], (ITERS + 1,), jnp.float32, 0.5, 1.5), 0.5, 1.5)
    col_basis = centred(part_splits[2], (POINTS, RANK), CLUSTER ** -0.5, 0.375, ((0, 16),))
    row_basis = centred(part_splits[3], (POINTS, RANK), (16 * RANK * LEAF_DEV) ** -0.5, 0.0234375, ((0, 16),))
    near_tiles = centred(part_splits[4], (POINTS, 3 * CLUSTER), (48 * CLUSTER) ** -0.5, 0.0546875, ((0, 16),))
    coupling = centred(part_splits[5], (LEAVES, RANK, RANK), RANK ** -0.5, 0.75, ((0, 16),))
    far_rows_keys = jax.random.split(jax.random.fold_in(part_splits[6], 1), LEAVES // LEAF_DEV)
    far_rows_turns = jax.random.permutation(jax.random.fold_in(part_splits[6], 3), LEAVES // LEAF_DEV)
    far_rows = jax.vmap(lambda own, number: deal_out(jax.random.fold_in(part_splits[6], 2), own, number, LEAF_DEV, CLUSTERS, 1, SLOT_CAP, 2))(far_rows_keys, far_rows_turns).reshape((LEAVES, 1))
    far_cols = touch_ends(jax.random.randint(part_splits[7], (LEAVES,), 0, CLUSTERS), jax.random.fold_in(part_splits[7], 1), 0, CLUSTERS - 1).astype(jnp.int32)
    return dict(probes=probes, cheb_coef=cheb_coef, col_basis=col_basis, row_basis=row_basis, near_tiles=near_tiles, coupling=coupling, far_rows=far_rows, far_cols=far_cols)


def round_trip(values):
    return lax.optimization_barrier(values.astype(jnp.bfloat16)).astype(jnp.float32)


def reference(probes, cheb_coef, col_basis, row_basis, near_tiles, coupling, far_rows, far_cols):
    highest = lax.Precision.HIGHEST
    clusters = N_BLOCKS
    aggregated = jnp.zeros((clusters, clusters, RANK, RANK), jnp.float32)
    aggregated = aggregated.at[far_rows[:, 0], far_cols].add(coupling.astype(jnp.float32))
    col_part = col_basis.astype(jnp.float32).reshape(clusters, CLUSTER, RANK)
    row_part = row_basis.astype(jnp.float32).reshape(clusters, CLUSTER, RANK)
    tiles = near_tiles.astype(jnp.float32).reshape(clusters, CLUSTER, 3 * CLUSTER)
    t_now = probes.astype(jnp.float32)
    t_prev = jnp.zeros_like(t_now)
    estimate = cheb_coef[0] * t_now
    for turn in range(ITERS):
        current = round_trip(t_now).reshape(clusters, CLUSTER, PROBES)
        moments = round_trip(jnp.einsum("ncr,ncp->nrp", col_part, current, precision=highest))
        far_sum = round_trip(jnp.einsum("rcij,cjp->rip", aggregated, moments, precision=highest))
        padded = jnp.pad(current, ((1, 1), (0, 0), (0, 0)))
        windows = jnp.concatenate([padded[:-2], padded[1:-1], padded[2:]], axis=1)
        near = jnp.einsum("ncd,ndp->ncp", tiles, windows, precision=highest)
        image = near + jnp.einsum("ncr,nrp->ncp", row_part, far_sum, precision=highest)
        image = image.reshape(clusters * CLUSTER, PROBES)
        if turn == 0:
            t_next = image
        else:
            t_next = 2.0 * image - t_prev
        estimate = estimate + cheb_coef[turn + 1] * t_next
        t_prev = t_now
        t_now = t_next
    return estimate
```

```python
import functools

import jax
import jax.numpy as jnp
from jax import lax
from jax.experimental import pallas as pl
from jax.experimental.pallas import tpu as pltpu
from jax.sharding import PartitionSpec as P

ITERS = 4
MESH = pl.DeviceIdType.MESH


def steps(low, high, body):
    if high - low <= 8:
        for j in range(low, high):
            body(j)
    else:
        lax.fori_loop(low, high, lambda j, carry: (body(j), carry)[1], 0)


def chebyshev_kernel(
    count, coef, probes, col_basis, row_basis, near, local, out,
    moments, halo, current, partner_block, part_out, part_in, t_a, t_b,
    send_sem, recv_sem, halo_send, halo_recv, part_send, part_recv, block_sem,
):
    group = lax.axis_index("groups")
    me = lax.axis_index("blocks")
    chips = count // 2
    chip, core = me // 2, me % 2
    mate = me + 1 - 2 * core
    rank = row_basis.shape[1]

    def at(block):
        return (group, block)

    def plane(j):
        return 2 * lax.rem(chip + j, chips) + core

    barrier = pltpu.get_barrier_semaphore()

    def greet(block):
        pl.semaphore_signal(barrier, inc=1, device_id=at(block), device_id_type=MESH)

    steps(1, chips, lambda j: greet(plane(j)))
    greet(mate)
    far_side = me - 1 + 2 * core
    has_side = jnp.logical_and(far_side >= 0, far_side < count)

    @pl.when(has_side)
    def _():
        greet(far_side)

    pl.semaphore_wait(barrier, chips + jnp.where(has_side, 1, 0))

    has_left, has_right = me > 0, me < count - 1

    def remote(src, dst, sem_a, sem_b, block):
        return pltpu.make_async_remote_copy(
            src_ref=src, dst_ref=dst, send_sem=sem_a, recv_sem=sem_b,
            device_id=at(block), device_id_type=MESH,
        )

    def moment_copy(k, j):
        return remote(
            moments.at[k, chip], moments.at[k, chip], send_sem.at[k, j], recv_sem.at[k, j], plane(j)
        )

    def moment_arrival(k, j):
        source = lax.rem(chip + chips - j, chips)
        return remote(
            moments.at[k, source], moments.at[k, source], send_sem.at[k, j], recv_sem.at[k, j], plane(j)
        )

    def halo_copy(k, side):
        target = me + 1 if side == 0 else me - 1
        return remote(
            current.at[k], halo.at[k, side], halo_send.at[k, side], halo_recv.at[k, side], target
        )

    def part_copy(k):
        return remote(part_out.at[k], part_in.at[k], part_send.at[k], part_recv.at[k], mate)

    block_copy = remote(
        local.at[1 - core], partner_block, block_sem.at[0], block_sem.at[1], mate
    )

    @pl.when(jnp.logical_not(has_left))
    def _():
        for k in range(ITERS):
            halo[k, 0] = jnp.zeros(halo.shape[2:], halo.dtype)

    @pl.when(jnp.logical_not(has_right))
    def _():
        for k in range(ITERS):
            halo[k, 1] = jnp.zeros(halo.shape[2:], halo.dtype)

    rows = probes.shape[0]
    first = probes[...].astype(jnp.float32)
    t_a[...] = first
    out[...] = coef[0] * first
    for k in range(ITERS):
        now = t_a if k % 2 == 0 else t_b
        other = t_b if k % 2 == 0 else t_a
        cur = probes[...] if k == 0 else now[...].astype(jnp.bfloat16)
        current[k] = cur
        moments[k, chip] = lax.dot_general(
            col_basis[...], cur, (((0,), (0,)), ((), ())), preferred_element_type=jnp.float32
        ).astype(jnp.bfloat16)
        steps(1, chips, lambda j: moment_copy(k, j).start())

        @pl.when(has_right)
        def _():
            halo_copy(k, 0).start()

        @pl.when(has_left)
        def _():
            halo_copy(k, 1).start()

        if k == 0:
            block_copy.start()

        image = jnp.dot(
            near[:, rows : 2 * rows], current[k], preferred_element_type=jnp.float32
        )
        if k == 0:
            block_copy.wait()
        steps(1, chips, lambda j: moment_arrival(k, j).wait_recv())
        whole = moments[k].reshape(chips * rank, probes.shape[1])
        part_out[k] = jnp.dot(partner_block[...], whole, preferred_element_type=jnp.float32)
        part_copy(k).start()
        own = jnp.dot(local[core], whole, preferred_element_type=jnp.float32)

        @pl.when(has_left)
        def _():
            halo_copy(k, 0).wait_recv()

        image += jnp.dot(near[:, :rows], halo[k, 0], preferred_element_type=jnp.float32)

        @pl.when(has_right)
        def _():
            halo_copy(k, 1).wait_recv()

        image += jnp.dot(near[:, 2 * rows :], halo[k, 1], preferred_element_type=jnp.float32)
        part_copy(k).wait_recv()
        far = (own + part_in[k]).astype(jnp.bfloat16)
        image += jnp.dot(row_basis[...], far, preferred_element_type=jnp.float32)
        t_next = image if k == 0 else 2.0 * image - other[...]
        if k < ITERS - 1:
            other[...] = t_next
        out[...] += coef[k + 1] * t_next

    for k in range(ITERS):
        steps(1, chips, lambda j: moment_copy(k, j).wait_send())

        @pl.when(has_right)
        def _():
            halo_copy(k, 0).wait_send()

        @pl.when(has_left)
        def _():
            halo_copy(k, 1).wait_send()

        part_copy(k).wait_send()


def shards(probes, cheb_coef, col_basis, row_basis, near_tiles, coupling, far_rows, far_cols):
    leaf_count, rank = coupling.shape[0], coupling.shape[1]
    rows, width = probes.shape
    count = lax.axis_size("blocks")
    chips = count // 2
    cap = 2 * leaf_count // count
    ids = far_rows[:, 0]
    order = jnp.arange(leaf_count, dtype=jnp.int32)
    earlier = (ids[None, :] == ids[:, None]) & (order[None, :] < order[:, None])
    slot = ids * cap + jnp.sum(earlier.astype(jnp.int32), axis=1)
    place = (slot[None, :] == jnp.arange(count * cap, dtype=jnp.int32)[:, None]).astype(jnp.bfloat16)
    tag_width = -(-count // 128) * 128
    tags = (far_cols[:, None] == jnp.arange(tag_width, dtype=jnp.int32)[None, :]).astype(jnp.bfloat16)
    flat = jnp.concatenate([coupling.reshape(leaf_count, rank * rank), tags], axis=1)
    sent = jnp.dot(place, flat, preferred_element_type=jnp.float32).astype(jnp.bfloat16)
    got = lax.all_to_all(sent, "blocks", split_axis=0, concat_axis=0, tiled=True)
    mine = lax.dot_general(
        got[:, rank * rank : rank * rank + count], got[:, : rank * rank],
        (((0,), (0,)), ((), ())), preferred_element_type=jnp.float32,
    ).astype(jnp.bfloat16)
    local = mine.reshape(chips, 2, rank, rank).transpose(1, 2, 0, 3).reshape(2, rank, chips * rank)

    vmem = pl.BlockSpec(memory_space=pltpu.VMEM)
    dma = pltpu.SemaphoreType.DMA
    return pl.pallas_call(
        functools.partial(chebyshev_kernel, count),
        out_shape=jax.ShapeDtypeStruct((rows, width), jnp.float32),
        in_specs=[pl.BlockSpec(memory_space=pltpu.SMEM)] + [vmem] * 5,
        out_specs=vmem,
        scratch_shapes=[
            pltpu.VMEM((ITERS, chips, rank, width), jnp.bfloat16),
            pltpu.VMEM((ITERS, 2, rows, width), jnp.bfloat16),
            pltpu.VMEM((ITERS, rows, width), jnp.bfloat16),
            pltpu.VMEM((rank, chips * rank), jnp.bfloat16),
            pltpu.VMEM((ITERS, rank, width), jnp.float32),
            pltpu.VMEM((ITERS, rank, width), jnp.float32),
            pltpu.VMEM((rows, width), jnp.float32),
            pltpu.VMEM((rows, width), jnp.float32),
            dma((ITERS, chips)),
            dma((ITERS, chips)),
            dma((ITERS, 2)),
            dma((ITERS, 2)),
            dma((ITERS,)),
            dma((ITERS,)),
            dma((2,)),
        ],
        compiler_params=pltpu.CompilerParams(
            collective_id=0, has_side_effects=True, vmem_limit_bytes=32 * 1024 * 1024
        ),
    )(cheb_coef, probes, col_basis, row_basis, near_tiles, local)


def solution(mesh):
    return jax.shard_map(
        shards,
        mesh=mesh,
        in_specs=(
            P(("groups", "blocks"), None),
            P("groups"),
            P(("groups", "blocks"), None),
            P(("groups", "blocks"), None),
            P(("groups", "blocks"), None),
            P(("groups", "blocks"), None, None),
            P(("groups", "blocks"), None),
            P(("groups", "blocks")),
        ),
        out_specs=P(("groups", "blocks"), None),
        check_vma=False,
    )
```

```python
import functools

import jax
import jax.numpy as jnp
from jax import lax
from jax.experimental import pallas as pl
from jax.experimental.pallas import tpu as pltpu
from jax.sharding import PartitionSpec as P

ITERS = 4
MESH = pl.DeviceIdType.MESH


def steps(low, high, body):
    if high - low <= 8:
        for j in range(low, high):
            body(j)
    else:
        lax.fori_loop(low, high, lambda j, carry: (body(j), carry)[1], 0)


def remote(src, dst, send, recv, target):
    return pltpu.make_async_remote_copy(
        src_ref=src, dst_ref=dst, send_sem=send, recv_sem=recv,
        device_id=target, device_id_type=MESH,
    )


def position():
    group, me = lax.axis_index("groups"), lax.axis_index("blocks")
    return lambda block: (group, block), me


def greet(target):
    pl.semaphore_signal(
        pltpu.get_barrier_semaphore(), inc=1, device_id=target, device_id_type=MESH
    )


def moments_of(basis, cur):
    return lax.dot_general(
        basis, cur, (((0,), (0,)), ((), ())), preferred_element_type=jnp.float32
    ).astype(jnp.bfloat16)


def start_kernel(
    count, probes, col_basis, near, slots, got, moments, near_out,
    halo, send_sem, recv_sem, slot_send, slot_recv, halo_send, halo_recv,
):
    at, me = position()
    chips = count // 2
    pairs = chips // 2
    chip, core = me // 2, me % 2
    pair, side = chip // 2, chip % 2
    rows = probes.shape[0]

    def plane(j):
        return at(2 * lax.rem(chip + j, chips) + core)

    def line(j):
        return at(4 * lax.rem(pair + j, pairs) + 2 * side + core)

    has_left, has_right = me > 0, me < count - 1
    steps(1, chips, lambda j: greet(plane(j)))
    greet(at(me + 1 - 2 * core))
    outer = me - 1 + 2 * core
    has_outer = jnp.logical_and(outer >= 0, outer < count)

    @pl.when(has_outer)
    def _():
        greet(at(outer))

    moments[pair] = moments_of(col_basis[...], probes[...])

    @pl.when(jnp.logical_not(has_left))
    def _():
        halo[0] = jnp.zeros(probes.shape, halo.dtype)

    @pl.when(jnp.logical_not(has_right))
    def _():
        halo[1] = jnp.zeros(probes.shape, halo.dtype)

    pl.semaphore_wait(pltpu.get_barrier_semaphore(), chips + jnp.where(has_outer, 1, 0))

    def slot_copy(j):
        return remote(
            slots.at[lax.rem(chip + j, chips)], got.at[chip], slot_send.at[j], slot_recv.at[j], plane(j)
        )

    def slot_arrival(j):
        source = lax.rem(chip + chips - j, chips)
        return remote(slots.at[source], got.at[source], slot_send.at[j], slot_recv.at[j], plane(j))

    def moment_copy(j):
        return remote(moments.at[pair], moments.at[pair], send_sem.at[j], recv_sem.at[j], line(j))

    def moment_arrival(j):
        source = lax.rem(pair + pairs - j, pairs)
        return remote(moments.at[source], moments.at[source], send_sem.at[j], recv_sem.at[j], line(j))

    def halo_copy(way):
        target = me + 1 if way == 0 else me - 1
        return remote(probes, halo.at[way], halo_send.at[way], halo_recv.at[way], at(target))

    steps(1, chips, lambda j: slot_copy(j).start())

    @pl.when(has_right)
    def _():
        halo_copy(0).start()

    @pl.when(has_left)
    def _():
        halo_copy(1).start()

    steps(1, pairs, lambda j: moment_copy(j).start())
    got[chip] = slots[chip]
    near_out[...] = jnp.dot(
        near[:, rows : 2 * rows], probes[...], preferred_element_type=jnp.float32
    )

    @pl.when(has_left)
    def _():
        halo_copy(0).wait_recv()

    near_out[...] += jnp.dot(near[:, :rows], halo[0], preferred_element_type=jnp.float32)

    @pl.when(has_right)
    def _():
        halo_copy(1).wait_recv()

    near_out[...] += jnp.dot(near[:, 2 * rows :], halo[1], preferred_element_type=jnp.float32)
    steps(1, pairs, lambda j: moment_arrival(j).wait_recv())
    steps(1, chips, lambda j: slot_arrival(j).wait_recv())
    steps(1, pairs, lambda j: moment_copy(j).wait_send())
    steps(1, chips, lambda j: slot_copy(j).wait_send())

    @pl.when(has_right)
    def _():
        halo_copy(0).wait_send()

    @pl.when(has_left)
    def _():
        halo_copy(1).wait_send()


def chebyshev_kernel(
    count, coef, probes, col_basis, row_basis, near, pieces, moments_0, near_0, out,
    moments, halo, current, blocks, local, part_out, part_in, t_a, t_b,
    send_sem, recv_sem, halo_send, halo_recv, part_send, part_recv, block_send, block_recv,
):
    at, me = position()
    pairs = count // 4
    pair, quarter = me // 4, me % 4
    rows, width = probes.shape
    rank = row_basis.shape[1]

    def line(j):
        return at(4 * lax.rem(pair + j, pairs) + quarter)

    def beside(j):
        return lax.rem(quarter + j, 4)

    def room(j):
        return at(4 * pair + beside(j))

    has_left, has_right = me > 0, me < count - 1
    steps(1, pairs, lambda j: greet(line(j)))
    steps(1, 4, lambda j: greet(room(j)))
    outer_left = jnp.logical_and(quarter == 0, has_left)
    outer_right = jnp.logical_and(quarter == 3, has_right)

    @pl.when(outer_left)
    def _():
        greet(at(me - 1))

    @pl.when(outer_right)
    def _():
        greet(at(me + 1))

    @pl.when(jnp.logical_not(has_left))
    def _():
        for k in range(1, ITERS):
            halo[k, 0] = jnp.zeros(probes.shape, halo.dtype)

    @pl.when(jnp.logical_not(has_right))
    def _():
        for k in range(1, ITERS):
            halo[k, 1] = jnp.zeros(probes.shape, halo.dtype)

    extra = jnp.where(jnp.logical_or(outer_left, outer_right), 1, 0)
    pl.semaphore_wait(pltpu.get_barrier_semaphore(), pairs + 2 + extra)

    def moment_copy(k, j):
        return remote(
            moments.at[k, pair], moments.at[k, pair], send_sem.at[k, j], recv_sem.at[k, j], line(j)
        )

    def moment_arrival(k, j):
        source = lax.rem(pair + pairs - j, pairs)
        return remote(
            moments.at[k, source], moments.at[k, source], send_sem.at[k, j], recv_sem.at[k, j], line(j)
        )

    def halo_copy(k, way):
        target = me + 1 if way == 0 else me - 1
        return remote(
            current.at[k], halo.at[k, way], halo_send.at[k, way], halo_recv.at[k, way], at(target)
        )

    def part_copy(k, j):
        return remote(
            part_out.at[k, beside(j)], part_in.at[k, quarter], part_send.at[k, j], part_recv.at[k, j], room(j)
        )

    def part_arrival(k, j):
        source = beside(4 - j)
        return remote(
            part_out.at[k, source], part_in.at[k, source], part_send.at[k, j], part_recv.at[k, j], room(j)
        )

    def block_copy(j):
        return remote(
            pieces.at[beside(j)], blocks.at[quarter], block_send.at[j], block_recv.at[j], room(j)
        )

    def block_arrival(j):
        source = beside(4 - j)
        return remote(pieces.at[source], blocks.at[source], block_send.at[j], block_recv.at[j], room(j))

    steps(1, 4, lambda j: block_copy(j).start())
    blocks[quarter] = pieces[quarter]
    first = probes[...].astype(jnp.float32)
    t_a[...] = first
    out[...] = coef[0] * first
    steps(1, 4, lambda j: block_arrival(j).wait_recv())
    half = 2 * rank
    for s in range(2):
        local[s * half : (s + 1) * half, :] = (
            blocks[2 * s].astype(jnp.float32) + blocks[2 * s + 1].astype(jnp.float32)
        ).astype(jnp.bfloat16)

    for k in range(ITERS):
        now = t_a if k % 2 == 0 else t_b
        other = t_b if k % 2 == 0 else t_a
        if k > 0:
            cur = now[...].astype(jnp.bfloat16)
            moments[k, pair] = moments_of(col_basis[...], cur)
            steps(1, pairs, lambda j: moment_copy(k, j).start())
            current[k] = cur

            @pl.when(has_right)
            def _():
                halo_copy(k, 0).start()

            @pl.when(has_left)
            def _():
                halo_copy(k, 1).start()

            near_out = jnp.dot(
                near[:, rows : 2 * rows], current[k], preferred_element_type=jnp.float32
            )
            steps(1, pairs, lambda j: moment_arrival(k, j).wait_recv())
            held = moments[k]
        else:
            held = moments_0[...]
            near_out = near_0[...]
        parts = jnp.dot(
            local[...], held.reshape(pairs * rank, width), preferred_element_type=jnp.float32
        )
        part_out[k] = parts.astype(jnp.bfloat16).reshape(4, rank, width)
        steps(1, 4, lambda j: part_copy(k, j).start())
        part_in[k, quarter] = part_out[k, quarter]
        if k > 0:

            @pl.when(has_left)
            def _():
                halo_copy(k, 0).wait_recv()

            near_out += jnp.dot(near[:, :rows], halo[k, 0], preferred_element_type=jnp.float32)

            @pl.when(has_right)
            def _():
                halo_copy(k, 1).wait_recv()

            near_out += jnp.dot(near[:, 2 * rows :], halo[k, 1], preferred_element_type=jnp.float32)
        steps(1, 4, lambda j: part_arrival(k, j).wait_recv())
        far = jnp.sum(part_in[k].astype(jnp.float32), axis=0).astype(jnp.bfloat16)
        image = near_out + jnp.dot(row_basis[...], far, preferred_element_type=jnp.float32)
        t_next = image if k == 0 else 2.0 * image - other[...]
        if k < ITERS - 1:
            other[...] = t_next
        out[...] += coef[k + 1] * t_next

    steps(1, 4, lambda j: block_copy(j).wait_send())
    for k in range(ITERS):
        if k > 0:
            steps(1, pairs, lambda j: moment_copy(k, j).wait_send())

            @pl.when(has_right)
            def _():
                halo_copy(k, 0).wait_send()

            @pl.when(has_left)
            def _():
                halo_copy(k, 1).wait_send()

        steps(1, 4, lambda j: part_copy(k, j).wait_send())


def shards(probes, cheb_coef, col_basis, row_basis, near_tiles, coupling, far_rows, far_cols):
    leaf_count, rank = coupling.shape[0], coupling.shape[1]
    rows, width = probes.shape
    count = lax.axis_size("blocks")
    chips, pairs = count // 2, count // 4
    cap = 2 * leaf_count // count
    depth = -(-2 * cap // 16) * 16
    ids = far_rows[:, 0]
    order = jnp.arange(leaf_count, dtype=jnp.int32)
    earlier = (ids[None, :] == ids[:, None]) & (order[None, :] < order[:, None])
    nth = jnp.sum(earlier.astype(jnp.int32), axis=1)
    slot = (ids // 2) * depth + (ids % 2) * cap + nth
    place = (slot[None, :] == jnp.arange(chips * depth, dtype=jnp.int32)[:, None]).astype(jnp.bfloat16)
    tag_width = -(-2 * count // 128) * 128
    tag = (ids % 2) * count + far_cols
    tags = (tag[:, None] == jnp.arange(tag_width, dtype=jnp.int32)[None, :]).astype(jnp.bfloat16)
    flat = jnp.concatenate([coupling.reshape(leaf_count, rank * rank), tags], axis=1)
    sent = jnp.dot(place, flat, preferred_element_type=jnp.float32).astype(jnp.bfloat16)
    sent = sent.reshape(chips, depth, flat.shape[1])

    vmem = pl.BlockSpec(memory_space=pltpu.VMEM)
    dma = pltpu.SemaphoreType.DMA
    grant = 48 * 1024 * 1024
    got, moments_0, near_0 = pl.pallas_call(
        functools.partial(start_kernel, count),
        out_shape=[
            jax.ShapeDtypeStruct(sent.shape, jnp.bfloat16),
            jax.ShapeDtypeStruct((pairs, rank, width), jnp.bfloat16),
            jax.ShapeDtypeStruct((rows, width), jnp.float32),
        ],
        in_specs=[vmem] * 4,
        out_specs=[vmem] * 3,
        scratch_shapes=[
            pltpu.VMEM((2, rows, width), jnp.bfloat16),
            dma((pairs,)), dma((pairs,)), dma((chips,)), dma((chips,)), dma((2,)), dma((2,)),
        ],
        compiler_params=pltpu.CompilerParams(
            collective_id=0, has_side_effects=True, vmem_limit_bytes=grant
        ),
    )(probes, col_basis, near_tiles, sent)

    got = got.reshape(chips * depth, flat.shape[1])
    mine = lax.dot_general(
        got[:, rank * rank : rank * rank + 2 * count], got[:, : rank * rank],
        (((0,), (0,)), ((), ())), preferred_element_type=jnp.float32,
    ).astype(jnp.bfloat16)
    pieces = mine.reshape(2, pairs, 4, rank, rank).transpose(2, 0, 3, 1, 4)
    pieces = pieces.reshape(4, 2 * rank, pairs * rank)

    return pl.pallas_call(
        functools.partial(chebyshev_kernel, count),
        out_shape=jax.ShapeDtypeStruct((rows, width), jnp.float32),
        in_specs=[pl.BlockSpec(memory_space=pltpu.SMEM)] + [vmem] * 7,
        out_specs=vmem,
        scratch_shapes=[
            pltpu.VMEM((ITERS, pairs, rank, width), jnp.bfloat16),
            pltpu.VMEM((ITERS, 2, rows, width), jnp.bfloat16),
            pltpu.VMEM((ITERS, rows, width), jnp.bfloat16),
            pltpu.VMEM((4, 2 * rank, pairs * rank), jnp.bfloat16),
            pltpu.VMEM((4 * rank, pairs * rank), jnp.bfloat16),
            pltpu.VMEM((ITERS, 4, rank, width), jnp.bfloat16),
            pltpu.VMEM((ITERS, 4, rank, width), jnp.bfloat16),
            pltpu.VMEM((rows, width), jnp.float32),
            pltpu.VMEM((rows, width), jnp.float32),
            dma((ITERS, pairs)), dma((ITERS, pairs)), dma((ITERS, 2)), dma((ITERS, 2)),
            dma((ITERS, 4)), dma((ITERS, 4)), dma((4,)), dma((4,)),
        ],
        compiler_params=pltpu.CompilerParams(
            collective_id=1, has_side_effects=True, vmem_limit_bytes=grant
        ),
    )(cheb_coef, probes, col_basis, row_basis, near_tiles, pieces, moments_0, near_0)


def solution(mesh):
    return jax.shard_map(
        shards,
        mesh=mesh,
        in_specs=(
            P(("groups", "blocks"), None),
            P("groups"),
            P(("groups", "blocks"), None),
            P(("groups", "blocks"), None),
            P(("groups", "blocks"), None),
            P(("groups", "blocks"), None, None),
            P(("groups", "blocks"), None),
            P(("groups", "blocks")),
        ),
        out_specs=P(("groups", "blocks"), None),
        check_vma=False,
    )
```

```python
import functools

import jax
import jax.numpy as jnp
from jax import lax
from jax.experimental import pallas as pl
from jax.experimental.pallas import tpu as pltpu
from jax.sharding import PartitionSpec as P

ITERS = 4
LANES = 128
MESH = pl.DeviceIdType.MESH


def steps(low, high, body):
    if high - low <= 8:
        for j in range(low, high):
            body(j)
    else:
        lax.fori_loop(low, high, lambda j, carry: (body(j), carry)[1], 0)


def remote(src, dst, send, recv, target):
    return pltpu.make_async_remote_copy(
        src_ref=src, dst_ref=dst, send_sem=send, recv_sem=recv,
        device_id=target, device_id_type=MESH,
    )


def position():
    group, me = lax.axis_index("groups"), lax.axis_index("blocks")
    return lambda block: (group, block), me


def greet(target):
    pl.semaphore_signal(
        pltpu.get_barrier_semaphore(), inc=1, device_id=target, device_id_type=MESH
    )


def start_kernel(
    count, probes, col_basis, near, slots, got, moments, near_out, basis_t,
    halo, send_sem, recv_sem, slot_send, slot_recv, halo_send, halo_recv,
    mate_sem,
):
    at, me = position()
    chips = count // 2
    pairs = chips // 2
    chip, core = me // 2, me % 2
    pair, side = chip // 2, chip % 2
    rows = probes.shape[0]

    def plane(j):
        return at(2 * lax.rem(chip + j, chips) + core)

    mate = at(me + 1 - 2 * core)
    has_left, has_right = me > 0, me < count - 1
    steps(1, chips, lambda j: greet(plane(j)))
    greet(mate)
    outer = me - 1 + 2 * core
    has_outer = jnp.logical_and(outer >= 0, outer < count)

    @pl.when(has_outer)
    def _():
        greet(at(outer))

    basis_t[...] = col_basis[...].T
    moments[core, side, pair] = jnp.dot(
        basis_t[...], probes[...], preferred_element_type=jnp.float32
    ).astype(jnp.bfloat16)

    @pl.when(jnp.logical_not(has_left))
    def _():
        halo[0] = jnp.zeros(probes.shape, halo.dtype)

    @pl.when(jnp.logical_not(has_right))
    def _():
        halo[1] = jnp.zeros(probes.shape, halo.dtype)

    pl.semaphore_wait(pltpu.get_barrier_semaphore(), chips + jnp.where(has_outer, 1, 0))

    def slot_copy(j):
        return remote(
            slots.at[lax.rem(chip + j, chips)], got.at[chip], slot_send.at[j], slot_recv.at[j], plane(j)
        )

    def slot_arrival(j):
        source = lax.rem(chip + chips - j, chips)
        return remote(slots.at[source], got.at[source], slot_send.at[j], slot_recv.at[j], plane(j))

    def moment_copy(j):
        own = moments.at[core, side, pair]
        return remote(own, own, send_sem.at[j], recv_sem.at[j], plane(j))

    def moment_arrival(j):
        source = lax.rem(chip + chips - j, chips)
        held = moments.at[core, lax.rem(source, 2), source // 2]
        return remote(held, held, send_sem.at[j], recv_sem.at[j], plane(j))

    mate_copy = remote(moments.at[core], moments.at[core], mate_sem.at[0], mate_sem.at[1], mate)
    mate_arrival = remote(
        moments.at[1 - core], moments.at[1 - core], mate_sem.at[0], mate_sem.at[1], mate
    )

    def halo_copy(way):
        target = me + 1 if way == 0 else me - 1
        return remote(probes, halo.at[way], halo_send.at[way], halo_recv.at[way], at(target))

    steps(1, chips, lambda j: moment_copy(j).start())
    steps(1, chips, lambda j: slot_copy(j).start())

    @pl.when(has_right)
    def _():
        halo_copy(0).start()

    @pl.when(has_left)
    def _():
        halo_copy(1).start()

    got[chip] = slots[chip]
    steps(1, chips, lambda j: moment_arrival(j).wait_recv())
    mate_copy.start()
    near_out[...] = jnp.dot(
        near[:, rows : 2 * rows], probes[...], preferred_element_type=jnp.float32
    )

    @pl.when(has_left)
    def _():
        halo_copy(0).wait_recv()

    near_out[...] += jnp.dot(near[:, :rows], halo[0], preferred_element_type=jnp.float32)

    @pl.when(has_right)
    def _():
        halo_copy(1).wait_recv()

    near_out[...] += jnp.dot(near[:, 2 * rows :], halo[1], preferred_element_type=jnp.float32)
    mate_arrival.wait_recv()
    steps(1, chips, lambda j: slot_arrival(j).wait_recv())
    mate_copy.wait_send()
    steps(1, chips, lambda j: moment_copy(j).wait_send())
    steps(1, chips, lambda j: slot_copy(j).wait_send())

    @pl.when(has_right)
    def _():
        halo_copy(0).wait_send()

    @pl.when(has_left)
    def _():
        halo_copy(1).wait_send()


def chebyshev_kernel(
    count, coef, probes, basis_t, row_basis, near, pieces, moments_0, near_0, out,
    moments, halo, current, blocks, local, part_out, part_in, t_a, t_b, near_sum,
    send_sem, recv_sem, halo_send, halo_recv, part_send, part_recv, block_send, block_recv,
):
    at, me = position()
    pairs = count // 4
    pair, quarter = me // 4, me % 4
    rows, width = probes.shape
    rank = row_basis.shape[1]
    lanes = current.shape[2]
    streams = width // lanes

    def line(j):
        return at(4 * lax.rem(pair + j, pairs) + quarter)

    def beside(j):
        return lax.rem(quarter + j, 4)

    def room(j):
        return at(4 * pair + beside(j))

    has_left, has_right = me > 0, me < count - 1
    steps(1, pairs, lambda j: greet(line(j)))
    steps(1, 4, lambda j: greet(room(j)))
    outer_left = jnp.logical_and(quarter == 0, has_left)
    outer_right = jnp.logical_and(quarter == 3, has_right)

    @pl.when(outer_left)
    def _():
        greet(at(me - 1))

    @pl.when(outer_right)
    def _():
        greet(at(me + 1))

    @pl.when(jnp.logical_not(has_left))
    def _():
        for q in range(streams, ITERS * streams):
            halo[q, 0] = jnp.zeros(halo.shape[2:], halo.dtype)

    @pl.when(jnp.logical_not(has_right))
    def _():
        for q in range(streams, ITERS * streams):
            halo[q, 1] = jnp.zeros(halo.shape[2:], halo.dtype)

    extra = jnp.where(jnp.logical_or(outer_left, outer_right), 1, 0)
    pl.semaphore_wait(pltpu.get_barrier_semaphore(), pairs + 2 + extra)

    def moment_copy(q, j):
        return remote(
            moments.at[q, pair], moments.at[q, pair], send_sem.at[q, j], recv_sem.at[q, j], line(j)
        )

    def moment_arrival(q, j):
        source = lax.rem(pair + pairs - j, pairs)
        return remote(
            moments.at[q, source], moments.at[q, source], send_sem.at[q, j], recv_sem.at[q, j], line(j)
        )

    def halo_copy(q, way):
        target = me + 1 if way == 0 else me - 1
        return remote(
            current.at[q], halo.at[q, way], halo_send.at[q, way], halo_recv.at[q, way], at(target)
        )

    def part_copy(q, j):
        return remote(
            part_out.at[q, beside(j)], part_in.at[q, quarter], part_send.at[q, j], part_recv.at[q, j], room(j)
        )

    def part_arrival(q, j):
        source = beside(4 - j)
        return remote(
            part_out.at[q, source], part_in.at[q, source], part_send.at[q, j], part_recv.at[q, j], room(j)
        )

    def block_copy(j):
        return remote(
            pieces.at[beside(j)], blocks.at[quarter], block_send.at[j], block_recv.at[j], room(j)
        )

    def block_arrival(j):
        source = beside(4 - j)
        return remote(pieces.at[source], blocks.at[source], block_send.at[j], block_recv.at[j], room(j))

    steps(1, 4, lambda j: block_copy(j).start())
    blocks[quarter] = pieces[quarter]
    first = probes[...].astype(jnp.float32)
    t_a[...] = first
    out[...] = coef[0] * first
    half = 2 * rank
    core = lax.rem(quarter, 2)
    mix = jnp.dot(
        basis_t[...], row_basis[...], preferred_element_type=jnp.float32
    ).astype(jnp.bfloat16)

    def gather_blocks():
        steps(1, 4, lambda j: block_arrival(j).wait_recv())
        for s in range(2):
            local[s * half : (s + 1) * half, :] = (
                blocks[2 * s].astype(jnp.float32) + blocks[2 * s + 1].astype(jnp.float32)
            ).astype(jnp.bfloat16)

    def mate_part(q):
        return remote(
            part_out.at[q, 1 - core], part_in.at[q, core], part_send.at[q, 0], part_recv.at[q, 0],
            at(me + 1 - 2 * core),
        )

    def mate_part_arrival(q):
        return remote(
            part_out.at[q, 1 - core], part_in.at[q, 1 - core], part_send.at[q, 0], part_recv.at[q, 0],
            at(me + 1 - 2 * core),
        )

    def columns(h):
        return slice(h * lanes, (h + 1) * lanes)

    def buffers(k):
        return (t_a, t_b) if k % 2 == 0 else (t_b, t_a)

    def part_stage(k, h):
        q = k * streams + h
        if k == 0:
            parts = jnp.zeros((half, lanes), jnp.float32)
            for c in range(4):
                held = moments_0[c % 2, c // 2, :, :, columns(h)]
                parts += jnp.dot(
                    pieces[c], held.reshape(pairs * rank, lanes), preferred_element_type=jnp.float32
                )
            part_out[q, 0:2] = parts.astype(jnp.bfloat16).reshape(2, rank, lanes)
            mate_part(q).start()
            part_in[q, core] = part_out[q, core]
        else:
            steps(1, pairs, lambda j: moment_arrival(q, j).wait_recv())
            parts = jnp.dot(
                local[...], moments[q].reshape(pairs * rank, lanes), preferred_element_type=jnp.float32
            )
            part_out[q] = parts.astype(jnp.bfloat16).reshape(4, rank, lanes)
            steps(1, 4, lambda j: part_copy(q, j).start())
            part_in[q, quarter] = part_out[q, quarter]
            near_sum[:, columns(h)] = jnp.dot(
                near[:, rows : 2 * rows], current[q], preferred_element_type=jnp.float32
            )

    def finish_stage(k, h):
        q = k * streams + h
        other = buffers(k)[1]
        if k > 0:
            near_out = near_sum[:, columns(h)]

            @pl.when(has_left)
            def _():
                halo_copy(q, 0).wait_recv()

            near_out += jnp.dot(near[:, :rows], halo[q, 0], preferred_element_type=jnp.float32)

            @pl.when(has_right)
            def _():
                halo_copy(q, 1).wait_recv()

            near_out += jnp.dot(near[:, 2 * rows :], halo[q, 1], preferred_element_type=jnp.float32)
            near_out = 2.0 * near_out - other[:, columns(h)]
        else:
            near_out = near_0[:, columns(h)]
        last = k == ITERS - 1
        if not last:
            later = q + streams
            base = jnp.dot(
                basis_t[...], near_out.astype(jnp.bfloat16), preferred_element_type=jnp.float32
            )
        if k == 0:
            mate_part_arrival(q).wait_recv()
            far = jnp.sum(part_in[q, 0:2].astype(jnp.float32), axis=0).astype(jnp.bfloat16)
            weight = 1.0
        else:
            steps(1, 4, lambda j: part_arrival(q, j).wait_recv())
            far = jnp.sum(part_in[q].astype(jnp.float32), axis=0).astype(jnp.bfloat16)
            weight = 2.0
        if not last:
            base += weight * jnp.dot(mix, far, preferred_element_type=jnp.float32)
            moments[later, pair] = base.astype(jnp.bfloat16)
            steps(1, pairs, lambda j: moment_copy(later, j).start())
        t_next = near_out + weight * jnp.dot(
            row_basis[...], far, preferred_element_type=jnp.float32
        )
        if not last:
            current[later] = t_next.astype(jnp.bfloat16)

            @pl.when(has_right)
            def _():
                halo_copy(later, 0).start()

            @pl.when(has_left)
            def _():
                halo_copy(later, 1).start()

            other[:, columns(h)] = t_next
        out[:, columns(h)] += coef[k + 1] * t_next

    for k in range(ITERS):
        if k == 1:
            gather_blocks()
        for h in range(streams):
            part_stage(k, h)
        for h in range(streams):
            finish_stage(k, h)

    steps(1, 4, lambda j: block_copy(j).wait_send())
    for q in range(ITERS * streams):
        if q >= streams:
            steps(1, pairs, lambda j: moment_copy(q, j).wait_send())

            @pl.when(has_right)
            def _():
                halo_copy(q, 0).wait_send()

            @pl.when(has_left)
            def _():
                halo_copy(q, 1).wait_send()

            steps(1, 4, lambda j: part_copy(q, j).wait_send())
        else:
            mate_part(q).wait_send()


def shards(probes, cheb_coef, col_basis, row_basis, near_tiles, coupling, far_rows, far_cols):
    leaf_count, rank = coupling.shape[0], coupling.shape[1]
    rows, width = probes.shape
    count = lax.axis_size("blocks")
    chips, pairs = count // 2, count // 4
    cap = 2 * leaf_count // count
    depth = -(-2 * cap // 16) * 16
    ids = far_rows[:, 0]
    order = jnp.arange(leaf_count, dtype=jnp.int32)
    earlier = (ids[None, :] == ids[:, None]) & (order[None, :] < order[:, None])
    nth = jnp.sum(earlier.astype(jnp.int32), axis=1)
    slot = (ids // 2) * depth + (ids % 2) * cap + nth
    place = (slot[None, :] == jnp.arange(chips * depth, dtype=jnp.int32)[:, None]).astype(jnp.bfloat16)
    tag_width = -(-2 * count // 128) * 128
    tag = (ids % 2) * count + far_cols
    tags = (tag[:, None] == jnp.arange(tag_width, dtype=jnp.int32)[None, :]).astype(jnp.bfloat16)
    flat = jnp.concatenate([coupling.reshape(leaf_count, rank * rank), tags], axis=1)
    sent = jnp.dot(place, flat, preferred_element_type=jnp.float32).astype(jnp.bfloat16)
    sent = sent.reshape(chips, depth, flat.shape[1])

    vmem = pl.BlockSpec(memory_space=pltpu.VMEM)
    dma = pltpu.SemaphoreType.DMA
    lanes = LANES
    turns = ITERS * (width // lanes)
    grant = 48 * 1024 * 1024
    got, moments_0, near_0, basis_t = pl.pallas_call(
        functools.partial(start_kernel, count),
        out_shape=[
            jax.ShapeDtypeStruct(sent.shape, jnp.bfloat16),
            jax.ShapeDtypeStruct((2, 2, pairs, rank, width), jnp.bfloat16),
            jax.ShapeDtypeStruct((rows, width), jnp.float32),
            jax.ShapeDtypeStruct((rank, rows), jnp.bfloat16),
        ],
        in_specs=[vmem] * 4,
        out_specs=[vmem] * 4,
        scratch_shapes=[
            pltpu.VMEM((2, rows, width), jnp.bfloat16),
            dma((chips,)), dma((chips,)), dma((chips,)), dma((chips,)), dma((2,)), dma((2,)), dma((2,)),
        ],
        compiler_params=pltpu.CompilerParams(
            collective_id=0, has_side_effects=True, vmem_limit_bytes=grant
        ),
    )(probes, col_basis, near_tiles, sent)

    got = got.reshape(chips * depth, flat.shape[1])
    mine = lax.dot_general(
        got[:, rank * rank : rank * rank + 2 * count], got[:, : rank * rank],
        (((0,), (0,)), ((), ())), preferred_element_type=jnp.float32,
    ).astype(jnp.bfloat16)
    pieces = mine.reshape(2, pairs, 4, rank, rank).transpose(2, 0, 3, 1, 4)
    pieces = pieces.reshape(4, 2 * rank, pairs * rank)

    return pl.pallas_call(
        functools.partial(chebyshev_kernel, count),
        out_shape=jax.ShapeDtypeStruct((rows, width), jnp.float32),
        in_specs=[pl.BlockSpec(memory_space=pltpu.SMEM)] + [vmem] * 7,
        out_specs=vmem,
        scratch_shapes=[
            pltpu.VMEM((turns, pairs, rank, lanes), jnp.bfloat16),
            pltpu.VMEM((turns, 2, rows, lanes), jnp.bfloat16),
            pltpu.VMEM((turns, rows, lanes), jnp.bfloat16),
            pltpu.VMEM((4, 2 * rank, pairs * rank), jnp.bfloat16),
            pltpu.VMEM((4 * rank, pairs * rank), jnp.bfloat16),
            pltpu.VMEM((turns, 4, rank, lanes), jnp.bfloat16),
            pltpu.VMEM((turns, 4, rank, lanes), jnp.bfloat16),
            pltpu.VMEM((rows, width), jnp.float32),
            pltpu.VMEM((rows, width), jnp.float32),
            pltpu.VMEM((rows, width), jnp.float32),
            dma((turns, pairs)), dma((turns, pairs)), dma((turns, 2)), dma((turns, 2)),
            dma((turns, 4)), dma((turns, 4)), dma((4,)), dma((4,)),
        ],
        compiler_params=pltpu.CompilerParams(
            collective_id=1, has_side_effects=True, vmem_limit_bytes=grant
        ),
    )(cheb_coef, probes, basis_t, row_basis, near_tiles, pieces, moments_0, near_0)


def solution(mesh):
    return jax.shard_map(
        shards,
        mesh=mesh,
        in_specs=(
            P(("groups", "blocks"), None),
            P("groups"),
            P(("groups", "blocks"), None),
            P(("groups", "blocks"), None),
            P(("groups", "blocks"), None),
            P(("groups", "blocks"), None, None),
            P(("groups", "blocks"), None),
            P(("groups", "blocks")),
        ),
        out_specs=P(("groups", "blocks"), None),
        check_vma=False,
    )
```

```python
import functools

import jax
import jax.numpy as jnp
from jax import lax
from jax.experimental import pallas as pl
from jax.experimental.pallas import tpu as pltpu
from jax.sharding import PartitionSpec as P

ITERS = 4
LANES = 128
MESH = pl.DeviceIdType.MESH


def steps(low, high, body):
    if high - low <= 8:
        for j in range(low, high):
            body(j)
    else:
        lax.fori_loop(low, high, lambda j, carry: (body(j), carry)[1], 0)


def remote(src, dst, send, recv, target):
    return pltpu.make_async_remote_copy(
        src_ref=src, dst_ref=dst, send_sem=send, recv_sem=recv,
        device_id=target, device_id_type=MESH,
    )


def position():
    group, me = lax.axis_index("groups"), lax.axis_index("blocks")
    return lambda block: (group, block), me


def greet(target):
    pl.semaphore_signal(
        pltpu.get_barrier_semaphore(), inc=1, device_id=target, device_id_type=MESH
    )


def start_kernel(
    count, probes, col_basis, near, slots, got, moments, near_out, basis_t,
    halo, send_sem, recv_sem, slot_send, slot_recv, halo_send, halo_recv,
    mate_sem,
):
    at, me = position()
    chips = count // 2
    pairs = chips // 2
    chip, core = me // 2, me % 2
    pair, side = chip // 2, chip % 2
    rows = probes.shape[0]

    def plane(j):
        return at(2 * lax.rem(chip + j, chips) + core)

    mate = at(me + 1 - 2 * core)
    has_left, has_right = me > 0, me < count - 1
    steps(1, chips, lambda j: greet(plane(j)))
    greet(mate)
    outer = me - 1 + 2 * core
    has_outer = jnp.logical_and(outer >= 0, outer < count)

    @pl.when(has_outer)
    def _():
        greet(at(outer))

    basis_t[...] = col_basis[...].T
    moments[core, side, pair] = jnp.dot(
        basis_t[...], probes[...], preferred_element_type=jnp.float32
    ).astype(jnp.bfloat16)

    @pl.when(jnp.logical_not(has_left))
    def _():
        halo[0] = jnp.zeros(probes.shape, halo.dtype)

    @pl.when(jnp.logical_not(has_right))
    def _():
        halo[1] = jnp.zeros(probes.shape, halo.dtype)

    pl.semaphore_wait(pltpu.get_barrier_semaphore(), chips + jnp.where(has_outer, 1, 0))

    def slot_copy(j):
        return remote(
            slots.at[lax.rem(chip + j, chips)], got.at[chip], slot_send.at[j], slot_recv.at[j], plane(j)
        )

    def slot_arrival(j):
        source = lax.rem(chip + chips - j, chips)
        return remote(slots.at[source], got.at[source], slot_send.at[j], slot_recv.at[j], plane(j))

    def moment_copy(j):
        own = moments.at[core, side, pair]
        return remote(own, own, send_sem.at[j], recv_sem.at[j], plane(j))

    def moment_arrival(j):
        source = lax.rem(chip + chips - j, chips)
        held = moments.at[core, lax.rem(source, 2), source // 2]
        return remote(held, held, send_sem.at[j], recv_sem.at[j], plane(j))

    mate_copy = remote(moments.at[core], moments.at[core], mate_sem.at[0], mate_sem.at[1], mate)
    mate_arrival = remote(
        moments.at[1 - core], moments.at[1 - core], mate_sem.at[0], mate_sem.at[1], mate
    )

    def halo_copy(way):
        target = me + 1 if way == 0 else me - 1
        return remote(probes, halo.at[way], halo_send.at[way], halo_recv.at[way], at(target))

    steps(1, chips, lambda j: moment_copy(j).start())
    if chips <= 8:
        for j in sorted(range(1, chips), key=lambda j: abs(2 * j - chips)):
            slot_copy(j).start()
    else:
        steps(1, chips, lambda j: slot_copy(j).start())

    @pl.when(has_right)
    def _():
        halo_copy(0).start()

    @pl.when(has_left)
    def _():
        halo_copy(1).start()

    got[chip] = slots[chip]
    steps(1, chips, lambda j: moment_arrival(j).wait_recv())
    mate_copy.start()
    near_out[...] = jnp.dot(
        near[:, rows : 2 * rows], probes[...], preferred_element_type=jnp.float32
    )

    @pl.when(has_left)
    def _():
        halo_copy(0).wait_recv()

    near_out[...] += jnp.dot(near[:, :rows], halo[0], preferred_element_type=jnp.float32)

    @pl.when(has_right)
    def _():
        halo_copy(1).wait_recv()

    near_out[...] += jnp.dot(near[:, 2 * rows :], halo[1], preferred_element_type=jnp.float32)
    mate_arrival.wait_recv()
    steps(1, chips, lambda j: slot_arrival(j).wait_recv())
    mate_copy.wait_send()
    steps(1, chips, lambda j: moment_copy(j).wait_send())
    steps(1, chips, lambda j: slot_copy(j).wait_send())

    @pl.when(has_right)
    def _():
        halo_copy(0).wait_send()

    @pl.when(has_left)
    def _():
        halo_copy(1).wait_send()


def chebyshev_kernel(
    count, coef, probes, basis_t, row_basis, near, pieces, moments_0, near_0, out,
    moments, halo, current, blocks, local, part_out, part_in, t_a, t_b, near_sum,
    send_sem, recv_sem, halo_send, halo_recv, part_send, part_recv, block_send, block_recv,
):
    at, me = position()
    pairs = count // 4
    pair, quarter = me // 4, me % 4
    rows, width = probes.shape
    rank = row_basis.shape[1]
    lanes = current.shape[2]
    streams = width // lanes

    def line(j):
        return at(4 * lax.rem(pair + j, pairs) + quarter)

    def beside(j):
        return lax.rem(quarter + j, 4)

    def room(j):
        return at(4 * pair + beside(j))

    has_left, has_right = me > 0, me < count - 1
    steps(1, pairs, lambda j: greet(line(j)))
    steps(1, 4, lambda j: greet(room(j)))
    outer_left = jnp.logical_and(quarter == 0, has_left)
    outer_right = jnp.logical_and(quarter == 3, has_right)

    @pl.when(outer_left)
    def _():
        greet(at(me - 1))

    @pl.when(outer_right)
    def _():
        greet(at(me + 1))

    @pl.when(jnp.logical_not(has_left))
    def _():
        for q in range(streams, ITERS * streams):
            halo[q, 0] = jnp.zeros(halo.shape[2:], halo.dtype)

    @pl.when(jnp.logical_not(has_right))
    def _():
        for q in range(streams, ITERS * streams):
            halo[q, 1] = jnp.zeros(halo.shape[2:], halo.dtype)

    extra = jnp.where(jnp.logical_or(outer_left, outer_right), 1, 0)
    pl.semaphore_wait(pltpu.get_barrier_semaphore(), pairs + 2 + extra)

    def moment_copy(q, j):
        return remote(
            moments.at[q, pair], moments.at[q, pair], send_sem.at[q, j], recv_sem.at[q, j], line(j)
        )

    def moment_arrival(q, j):
        source = lax.rem(pair + pairs - j, pairs)
        return remote(
            moments.at[q, source], moments.at[q, source], send_sem.at[q, j], recv_sem.at[q, j], line(j)
        )

    def halo_copy(q, way):
        target = me + 1 if way == 0 else me - 1
        return remote(
            current.at[q], halo.at[q, way], halo_send.at[q, way], halo_recv.at[q, way], at(target)
        )

    def part_copy(q, j):
        return remote(
            part_out.at[q, beside(j)], part_in.at[q, quarter], part_send.at[q, j], part_recv.at[q, j], room(j)
        )

    def part_arrival(q, j):
        source = beside(4 - j)
        return remote(
            part_out.at[q, source], part_in.at[q, source], part_send.at[q, j], part_recv.at[q, j], room(j)
        )

    def block_copy(j):
        return remote(
            pieces.at[beside(j)], blocks.at[quarter], block_send.at[j], block_recv.at[j], room(j)
        )

    def block_arrival(j):
        source = beside(4 - j)
        return remote(pieces.at[source], blocks.at[source], block_send.at[j], block_recv.at[j], room(j))

    steps(1, 4, lambda j: block_copy(j).start())
    blocks[quarter] = pieces[quarter]
    first = probes[...].astype(jnp.float32)
    t_a[...] = first
    out[...] = coef[0] * first
    half = 2 * rank
    core = lax.rem(quarter, 2)
    mix = jnp.dot(
        basis_t[...], row_basis[...], preferred_element_type=jnp.float32
    ).astype(jnp.bfloat16)

    def gather_blocks():
        steps(1, 4, lambda j: block_arrival(j).wait_recv())
        for s in range(2):
            local[s * half : (s + 1) * half, :] = (
                blocks[2 * s].astype(jnp.float32) + blocks[2 * s + 1].astype(jnp.float32)
            ).astype(jnp.bfloat16)

    def mate_part(q):
        return remote(
            part_out.at[q, 1 - core], part_in.at[q, core], part_send.at[q, 0], part_recv.at[q, 0],
            at(me + 1 - 2 * core),
        )

    def mate_part_arrival(q):
        return remote(
            part_out.at[q, 1 - core], part_in.at[q, 1 - core], part_send.at[q, 0], part_recv.at[q, 0],
            at(me + 1 - 2 * core),
        )

    def columns(h):
        return slice(h * lanes, (h + 1) * lanes)

    def buffers(k):
        return (t_a, t_b) if k % 2 == 0 else (t_b, t_a)

    def part_stage(k, h):
        q = k * streams + h
        if k == 0:
            parts = jnp.zeros((half, lanes), jnp.float32)
            for c in range(4):
                held = moments_0[c % 2, c // 2, :, :, columns(h)]
                parts += jnp.dot(
                    pieces[c], held.reshape(pairs * rank, lanes), preferred_element_type=jnp.float32
                )
            part_out[q, 0:2] = parts.astype(jnp.bfloat16).reshape(2, rank, lanes)
            mate_part(q).start()
            part_in[q, core] = part_out[q, core]
        else:
            steps(1, pairs, lambda j: moment_arrival(q, j).wait_recv())
            parts = jnp.dot(
                local[...], moments[q].reshape(pairs * rank, lanes), preferred_element_type=jnp.float32
            )
            part_out[q] = parts.astype(jnp.bfloat16).reshape(4, rank, lanes)
            steps(1, 4, lambda j: part_copy(q, j).start())
            part_in[q, quarter] = part_out[q, quarter]
            near_sum[:, columns(h)] = jnp.dot(
                near[:, rows : 2 * rows], current[q], preferred_element_type=jnp.float32
            )

    def finish_stage(k, h):
        q = k * streams + h
        other = buffers(k)[1]
        if k > 0:
            near_out = near_sum[:, columns(h)]

            @pl.when(has_left)
            def _():
                halo_copy(q, 0).wait_recv()

            near_out += jnp.dot(near[:, :rows], halo[q, 0], preferred_element_type=jnp.float32)

            @pl.when(has_right)
            def _():
                halo_copy(q, 1).wait_recv()

            near_out += jnp.dot(near[:, 2 * rows :], halo[q, 1], preferred_element_type=jnp.float32)
            near_out = 2.0 * near_out - other[:, columns(h)]
        else:
            near_out = near_0[:, columns(h)]
        last = k == ITERS - 1
        if not last:
            later = q + streams
            base = jnp.dot(
                basis_t[...], near_out.astype(jnp.bfloat16), preferred_element_type=jnp.float32
            )
        if k == 0:
            mate_part_arrival(q).wait_recv()
            far = jnp.sum(part_in[q, 0:2].astype(jnp.float32), axis=0).astype(jnp.bfloat16)
            weight = 1.0
        else:
            steps(1, 4, lambda j: part_arrival(q, j).wait_recv())
            far = jnp.sum(part_in[q].astype(jnp.float32), axis=0).astype(jnp.bfloat16)
            weight = 2.0
        if not last:
            base += weight * jnp.dot(mix, far, preferred_element_type=jnp.float32)
            moments[later, pair] = base.astype(jnp.bfloat16)
            steps(1, pairs, lambda j: moment_copy(later, j).start())
        t_next = near_out + weight * jnp.dot(
            row_basis[...], far, preferred_element_type=jnp.float32
        )
        if not last:
            current[later] = t_next.astype(jnp.bfloat16)

            @pl.when(has_right)
            def _():
                halo_copy(later, 0).start()

            @pl.when(has_left)
            def _():
                halo_copy(later, 1).start()

            other[:, columns(h)] = t_next
        out[:, columns(h)] += coef[k + 1] * t_next

    for k in range(ITERS):
        if k == 1:
            gather_blocks()
        for h in range(streams):
            part_stage(k, h)
        for h in range(streams):
            finish_stage(k, h)

    steps(1, 4, lambda j: block_copy(j).wait_send())
    for q in range(ITERS * streams):
        if q >= streams:
            steps(1, pairs, lambda j: moment_copy(q, j).wait_send())

            @pl.when(has_right)
            def _():
                halo_copy(q, 0).wait_send()

            @pl.when(has_left)
            def _():
                halo_copy(q, 1).wait_send()

            steps(1, 4, lambda j: part_copy(q, j).wait_send())
        else:
            mate_part(q).wait_send()


def shards(probes, cheb_coef, col_basis, row_basis, near_tiles, coupling, far_rows, far_cols):
    leaf_count, rank = coupling.shape[0], coupling.shape[1]
    rows, width = probes.shape
    count = lax.axis_size("blocks")
    chips, pairs = count // 2, count // 4
    cap = 2 * leaf_count // count
    depth = -(-2 * cap // 16) * 16
    ids = far_rows[:, 0]
    order = jnp.arange(leaf_count, dtype=jnp.int32)
    earlier = (ids[None, :] == ids[:, None]) & (order[None, :] < order[:, None])
    nth = jnp.sum(earlier.astype(jnp.int32), axis=1)
    slot = (ids // 2) * depth + (ids % 2) * cap + nth
    place = (slot[None, :] == jnp.arange(chips * depth, dtype=jnp.int32)[:, None]).astype(jnp.bfloat16)
    tag_width = -(-2 * count // 128) * 128
    tag = (ids % 2) * count + far_cols
    tags = (tag[:, None] == jnp.arange(tag_width, dtype=jnp.int32)[None, :]).astype(jnp.bfloat16)
    flat = jnp.concatenate([coupling.reshape(leaf_count, rank * rank), tags], axis=1)
    sent = jnp.dot(place, flat, preferred_element_type=jnp.float32).astype(jnp.bfloat16)
    sent = sent.reshape(chips, depth, flat.shape[1])

    vmem = pl.BlockSpec(memory_space=pltpu.VMEM)
    dma = pltpu.SemaphoreType.DMA
    lanes = LANES
    turns = ITERS * (width // lanes)
    grant = 48 * 1024 * 1024
    got, moments_0, near_0, basis_t = pl.pallas_call(
        functools.partial(start_kernel, count),
        out_shape=[
            jax.ShapeDtypeStruct(sent.shape, jnp.bfloat16),
            jax.ShapeDtypeStruct((2, 2, pairs, rank, width), jnp.bfloat16),
            jax.ShapeDtypeStruct((rows, width), jnp.float32),
            jax.ShapeDtypeStruct((rank, rows), jnp.bfloat16),
        ],
        in_specs=[vmem] * 4,
        out_specs=[vmem] * 4,
        scratch_shapes=[
            pltpu.VMEM((2, rows, width), jnp.bfloat16),
            dma((chips,)), dma((chips,)), dma((chips,)), dma((chips,)), dma((2,)), dma((2,)), dma((2,)),
        ],
        compiler_params=pltpu.CompilerParams(
            collective_id=0, has_side_effects=True, vmem_limit_bytes=grant
        ),
    )(probes, col_basis, near_tiles, sent)

    got = got.reshape(chips * depth, flat.shape[1])
    mine = lax.dot_general(
        got[:, rank * rank : rank * rank + 2 * count], got[:, : rank * rank],
        (((0,), (0,)), ((), ())), preferred_element_type=jnp.float32,
    ).astype(jnp.bfloat16)
    pieces = mine.reshape(2, pairs, 4, rank, rank).transpose(2, 0, 3, 1, 4)
    pieces = pieces.reshape(4, 2 * rank, pairs * rank)

    return pl.pallas_call(
        functools.partial(chebyshev_kernel, count),
        out_shape=jax.ShapeDtypeStruct((rows, width), jnp.float32),
        in_specs=[pl.BlockSpec(memory_space=pltpu.SMEM)] + [vmem] * 7,
        out_specs=vmem,
        scratch_shapes=[
            pltpu.VMEM((turns, pairs, rank, lanes), jnp.bfloat16),
            pltpu.VMEM((turns, 2, rows, lanes), jnp.bfloat16),
            pltpu.VMEM((turns, rows, lanes), jnp.bfloat16),
            pltpu.VMEM((4, 2 * rank, pairs * rank), jnp.bfloat16),
            pltpu.VMEM((4 * rank, pairs * rank), jnp.bfloat16),
            pltpu.VMEM((turns, 4, rank, lanes), jnp.bfloat16),
            pltpu.VMEM((turns, 4, rank, lanes), jnp.bfloat16),
            pltpu.VMEM((rows, width), jnp.float32),
            pltpu.VMEM((rows, width), jnp.float32),
            pltpu.VMEM((rows, width), jnp.float32),
            dma((turns, pairs)), dma((turns, pairs)), dma((turns, 2)), dma((turns, 2)),
            dma((turns, 4)), dma((turns, 4)), dma((4,)), dma((4,)),
        ],
        compiler_params=pltpu.CompilerParams(
            collective_id=1, has_side_effects=True, vmem_limit_bytes=grant
        ),
    )(cheb_coef, probes, basis_t, row_basis, near_tiles, pieces, moments_0, near_0)


def solution(mesh):
    return jax.shard_map(
        shards,
        mesh=mesh,
        in_specs=(
            P(("groups", "blocks"), None),
            P("groups"),
            P(("groups", "blocks"), None),
            P(("groups", "blocks"), None),
            P(("groups", "blocks"), None),
            P(("groups", "blocks"), None, None),
            P(("groups", "blocks"), None),
            P(("groups", "blocks")),
        ),
        out_specs=P(("groups", "blocks"), None),
        check_vma=False,
    )
```
